32 devices in a mesh: space: 8 (over z, y), tm: 4 (over x, core).
Axes of the slice: x: 2, y: 2, z: 4, core: 2. Of those that a mesh axis runs over, the one named last changes fastest.
Arguments:
- initial: float32 [3, 32, 128, 128], P(None, 'space'), may hold values from -6 to 6
- guess: float32 [8, 3, 32, 128, 128], P('tm', None, 'space'), may hold values from -6 to 6
- coarse_map: float32 [3, 3, 32, 128, 128], P(None, None, 'space'), may hold values from -0.12 to 0.99
- sites: int32 [32, 128, 128], P('space'), may hold values from 0 to 127
- mobility: float32 [128], replicated, may hold values from 0.01 to 0.08
Outputs:
- corrected: float32 [8, 3, 32, 128, 128], P('tm', None, 'space')
The draws below stay inside these ranges and needn't reach their ends.
All inputs are finite; a program needn't handle non-finite values.
Results may differ from the reference program's by a relative error of at most 0.00002.
Values sent between devices are 32-bit elements; how exact they have to be, the bound alone decides.
A program may use at most 128 MiB of HBM per device.

```python
import math
import jax
import jax.numpy as jnp
from jax import lax

NY = 128
NX = 128
M = 16
ORIENT = 128
NZ = 32
K = 8


def draw_coarse_map(key, part):
    key_diag, key_off = jax.random.split(key)
    shape = (3, 3, NZ, NY, NX)
    diagonal = jax.random.uniform(key_diag, shape, jnp.float32, 0.3, 0.98)
    spread = jax.random.uniform(key_off, shape, jnp.float32, -0.12, 0.12)
    unit_map = jnp.eye(3, dtype=jnp.float32)[:, :, None, None, None]
    return unit_map * diagonal + (1.0 - unit_map) * spread


def touch_ends(values, stream_key, smallest, high):
    extent = values.shape
    index_at = [jax.random.randint(jax.random.fold_in(stream_key, axis), (), 0, extent[axis]) for axis in range(len(extent))]
    values = values.at[tuple(index_at)].set(smallest)
    longest = extent.index(max(extent))
    index_at[longest] = (index_at[longest] + 1) % extent[longest]
    return values.at[tuple(index_at)].set(high)


def levels(own_key, extent, cuts, low, top_value):
    gain = 1.0
    for dim, shards_of in cuts:
        heights = jax.random.uniform(jax.random.fold_in(jax.random.fold_in(own_key, 6), dim), (shards_of,), jnp.float32, low / len(cuts), top_value / len(cuts))
        gain = gain * jnp.repeat(jnp.exp(heights), extent[dim] // shards_of).reshape((-1,) + (1,) * (len(extent) - 1 - dim))
    return gain


def noise(rng, extent, deviation, most, pieces=(), kind=jnp.bfloat16):
    loudness = levels(rng, extent, pieces, -0.22, 0.18) if pieces else 1.0
    values = jax.random.normal(rng, extent, jnp.float32) * deviation * loudness
    return jnp.minimum(jnp.maximum(values, -most), most).astype(kind)


def setup_inputs(seed: int = 0) -> dict:
    seeds = jax.random.split(jax.random.key(seed), 6)
    return {
        "initial": noise(seeds[0], (3, NZ, NY, NX), 1.0, 6.0, ((1, 8),), jnp.float32),
        "guess": noise(seeds[1], (K, 3, NZ, NY, NX), 1.0, 6.0, ((0, 4), (2, 8)), jnp.float32),
        "coarse_map": draw_coarse_map(jax.random.fold_in(seeds[5], 71), 0),
        "sites": touch_ends(jax.random.randint(seeds[3], (NZ, NY, NX), 0, ORIENT), jax.random.fold_in(seeds[3], 1), 0, ORIENT - 1).astype(jnp.int32),
        "mobility": jnp.clip(jnp.exp(jax.random.uniform(seeds[4], (ORIENT,), jnp.float32, math.log(0.01), math.log(0.08))), 0.01, 0.08),
    }


diffusion_number = 0.15
heat_release = 0.5
hardening = 0.02
saturation = 2.0


def advance(fields, mobile):
    heat_field, density, progress = fields[0], fields[1], fields[2]
    padded = jnp.pad(heat_field, 1)
    laplace = padded[2:, 1:-1, 1:-1] + padded[:-2, 1:-1, 1:-1]
    laplace = laplace + padded[1:-1, 2:, 1:-1] + padded[1:-1, :-2, 1:-1]
    laplace = laplace + padded[1:-1, 1:-1, 2:] + padded[1:-1, 1:-1, :-2]
    laplace = laplace - 6.0 * heat_field
    driving = density * density / (1.0 + density * density)
    growth = mobile * (1.0 + 0.5 * jnp.tanh(heat_field)) * driving * (1.0 - jnp.tanh(progress))
    new_heat = heat_field + diffusion_number * laplace + heat_release * growth
    new_density = density + hardening * (saturation - density) - density * growth
    return jnp.stack([new_heat, new_density, progress + growth])


def propagate(fields, mobile):
    return lax.fori_loop(0, M, lambda step_count, value: advance(value, mobile), fields)


def apply_map(coarse, vector):
    return jnp.stack([coarse[row, 0] * vector[0] + coarse[row, 1] * vector[1] + coarse[row, 2] * vector[2] for row in range(3)])


def reference(initial, guess, coarse_map, sites, mobility):
    mobile = mobility[sites]
    lefts_old = jnp.concatenate([initial[None], guess[:-1]], 0)
    relaxed = lax.map(lambda value: propagate(value, mobile), lefts_old)
    lefts_new = jnp.concatenate([initial[None], relaxed[:-1]], 0)
    fine = lax.map(lambda value: propagate(value, mobile), lefts_new)

    def chain(incoming, pair):
        fine_value, left_value = pair
        defect = fine_value - apply_map(coarse_map, left_value)
        updated = apply_map(coarse_map, incoming) + defect
        return updated, updated

    final_value, corrected = lax.scan(chain, initial, (fine, lefts_new))
    return corrected
```

```python
import functools

import jax
import jax.numpy as jnp
from jax import lax
from jax.experimental import pallas as pl
from jax.experimental.pallas import tpu as pltpu
from jax.sharding import PartitionSpec as P

M = 16
PAD = 8
ROWS = 32
EDGE = 2
CHUNKS = 2
MESH = pl.DeviceIdType.MESH

diffusion_number = 0.15
heat_release = 0.5
hardening = 0.02
saturation = 2.0


def kernel(
    spaces, blocks,
    initial, guess, coarse, sites, mobility, out,
    heat_a, heat_b, heat_c, dens, prog, mobile, own_mobile,
    relaxed, relaxed_out, fine, arriving, maps,
    start_send, start_recv, local_sem, first_send, mob_send, mob_recv,
    halo_send, halo_recv, edge_send, edge_recv,
    relaxed_send, relaxed_recv, back_send, back_recv, chain_send, chain_recv, map_sem,
):
    depth = sites.shape[0]
    ny, nx = sites.shape[1], sites.shape[2]
    s, t = lax.axis_index("space"), lax.axis_index("tm")
    half = lax.rem(s, 2)
    first, last = t == 0, t == blocks - 1
    later = jnp.logical_not(first)
    thick, stride = 2 * depth, 2
    offset = half * depth
    other = 1 - half
    base = s - half
    partner = base + other
    has_low, has_high = s >= stride, s < spaces - stride
    rows = pl.ds(PAD, ny)

    barrier = pltpu.get_barrier_semaphore()

    def place(space, tm):
        return {"space": space, "tm": tm}

    zero_rows = jnp.zeros((PAD, nx), jnp.float32)
    for heat in (heat_a, heat_b, heat_c):
        for layer in range(2 * depth + 4):
            heat[layer, pl.ds(0, PAD), :] = zero_rows
            heat[layer, pl.ds(PAD + ny, PAD), :] = zero_rows
        for layer in (0, 1, thick + 2, thick + 3):
            heat[layer, rows, :] = jnp.zeros((ny, nx), jnp.float32)

    friends = [
        (t >= 0, partner, t),
        (t > 0, base, t - 1), (t > 0, base + 1, t - 1),
        (t < blocks - 1, base, t + 1), (t < blocks - 1, base + 1, t + 1),
        (has_low, s - stride, t), (has_high, s + stride, t),
    ]
    count = 0
    for there, space, tm in friends:
        @pl.when(there)
        def _(space=space, tm=tm):
            pl.semaphore_signal(barrier, 1, device_id=place(space, tm), device_id_type=MESH)
        count = count + there.astype(jnp.int32)
    def piece_of(source, piece):
        if piece == 0:
            return source * (depth - EDGE), EDGE
        return (1 - source) * EDGE, depth - EDGE

    def landing(field, where, low, layers):
        start = where * depth + low
        if field == 0:
            return heat_a.at[pl.ds(start + 2, layers), rows, :]
        return (dens, prog)[field - 1].at[pl.ds(start + 1, layers)]

    def start_copy(source, chain, field, piece, tm):
        low, layers = piece_of(source, piece)
        return pltpu.make_async_remote_copy(
            guess.at[chain, field, pl.ds(low, layers)], landing(field, source, low, layers),
            start_send.at[chain, field, piece], start_recv.at[source, field, piece],
            device_id=place(base + chain, tm), device_id_type=MESH)

    def local_copy(field):
        return pltpu.make_async_copy(initial.at[field], landing(field, half, 0, depth), local_sem.at[field])

    def first_copy(source, field, piece):
        low, layers = piece_of(source, piece)
        return pltpu.make_async_remote_copy(
            initial.at[field, pl.ds(low, layers)], landing(field, source, low, layers),
            first_send.at[field, piece], start_recv.at[source, field, piece],
            device_id=place(partner, t), device_id_type=MESH)

    map_copy = pltpu.make_async_copy(coarse, maps, map_sem)

    @pl.when(first)
    def _():
        for field in range(3):
            local_copy(field).start()

    table = jnp.broadcast_to(mobility[...], (8, nx))

    def look_up(layer, carry):
        for row in range(0, ny, 8):
            index = sites[layer, pl.ds(row, 8), :]
            found = jnp.take_along_axis(table, index, axis=1, mode="promise_in_bounds")
            own_mobile[layer, pl.ds(row, 8), :] = found
            mobile[layer + 1 + offset, pl.ds(row, 8), :] = found
        return carry

    lax.fori_loop(0, depth, look_up, 0)
    mobile_copy = pltpu.make_async_remote_copy(
        own_mobile, mobile.at[pl.ds(1 + half * depth, depth)], mob_send, mob_recv,
        device_id=place(partner, t), device_id_type=MESH)
    pl.semaphore_wait(barrier, count)

    odd = lax.rem(t, 2) == 1
    deferred = jnp.logical_and(later, jnp.logical_not(odd))
    mobile_late = jnp.logical_or(first, jnp.logical_and(odd, t > 2))

    def send_start(go):
        @pl.when(jnp.logical_and(jnp.logical_not(last), go))
        def _():
            for piece in range(2):
                for field in range(3):
                    for chain in range(2):
                        start_copy(half, chain, field, piece, t + 1).start()

    def wait_sent(go):
        @pl.when(jnp.logical_and(jnp.logical_not(last), go))
        def _():
            for field in range(3):
                for chain in range(2):
                    for piece in range(2):
                        start_copy(half, chain, field, piece, t + 1).wait_send()

    def wait_start(piece):
        for field in range(3):
            start_copy(other, 0, field, piece, t).wait_recv()

        @pl.when(later)
        def _():
            for field in range(3):
                start_copy(half, 0, field, piece, t).wait_recv()

    send_start(jnp.logical_not(deferred))

    @pl.when(jnp.logical_not(mobile_late))
    def _():
        mobile_copy.start()

    map_copy.start()
    wait_sent(first)

    @pl.when(first)
    def _():
        for piece in range(2):
            for field in range(3):
                first_copy(half, field, piece).start()
        for field in range(3):
            local_copy(field).wait()

    wait_start(0)

    @pl.when(mobile_late)
    def _():
        mobile_copy.start()

    part = ny // CHUNKS

    def halo(heat, parity, side, far, chunk):
        source, target, space = (
            (2 + far, thick + 2 + far, s - stride), (thick + 1 - far, 1 - far, s + stride))[side]
        some = pl.ds(PAD + chunk * part, part)
        return pltpu.make_async_remote_copy(
            heat.at[source, some, :], heat.at[target, some, :],
            halo_send.at[parity, side, far, chunk], halo_recv.at[parity, side, far, chunk],
            device_id=place(space, t), device_id_type=MESH)

    def send_halo(heat, parity, side, far, chunk, go):
        @pl.when(jnp.logical_and((has_low, has_high)[side], go))
        def _():
            halo(heat, parity, side, far, chunk).start()

    def wait_halo(heat, parity, side, far, chunk):
        @pl.when((has_low, has_high)[side])
        def _():
            halo(heat, parity, side, far, chunk).wait_send()
            halo(heat, parity, 1 - side, far, chunk).wait_recv()

    for far in range(2):
        for side in range(2):
            for chunk in range(CHUNKS):
                send_halo(heat_a, 0, side, far, chunk, True)
    edges = (dens, prog, mobile)

    def edge(number, side):
        ref = edges[number]
        source, target, space = ((1, thick + 1, s - stride), (thick, 0, s + stride))[side]
        return pltpu.make_async_remote_copy(
            ref.at[source], ref.at[target], edge_send.at[number, side], edge_recv.at[number, side],
            device_id=place(space, t), device_id_type=MESH)

    def send_edges(numbers):
        for side in range(2):
            @pl.when((has_low, has_high)[side])
            def _(side=side):
                for number in numbers:
                    edge(number, side).start()

    send_edges((0, 1))

    mobile_copy.wait()

    send_edges((2,))

    wait_start(1)

    send_start(deferred)

    for side in range(2):
        @pl.when((has_low, has_high)[side])
        def _(side=side):
            for number in range(3):
                edge(number, side).wait_send()
                edge(number, 1 - side).wait_recv()

    lane = lax.broadcasted_iota(jnp.int32, (ROWS, nx), 1)
    not_first, not_last = lane > 0, lane < nx - 1

    def update(source, target, layer, skip=0):
        for row in range(0, ny, ROWS):
            here = pl.ds(row, ROWS)
            center = source[layer, pl.ds(PAD + row, ROWS), :]
            density = dens[layer - 1, here, :]
            progress = prog[layer - 1, here, :]
            square = density * density
            driving = square * pl.reciprocal(1.0 + square)
            growth = mobile[layer - 1, here, :] * (1.0 + 0.5 * jnp.tanh(center)) * driving
            growth = growth * (1.0 - jnp.tanh(progress))
            if target is not None:
                around = source[layer, pl.ds(PAD + row - 1, ROWS), :] + source[layer, pl.ds(PAD + row + 1, ROWS), :]
                if skip != -1:
                    around = around + source[layer - 1, pl.ds(PAD + row, ROWS), :]
                if skip != 1:
                    around = around + source[layer + 1, pl.ds(PAD + row, ROWS), :]
                left = jnp.where(not_first, pltpu.roll(center, 1, 1), 0.0)
                right = jnp.where(not_last, pltpu.roll(center, nx - 1, 1), 0.0)
                around = around + (left + right)
                target[layer, pl.ds(PAD + row, ROWS), :] = (
                    (1.0 - 6.0 * diffusion_number) * center + diffusion_number * around + heat_release * growth)
            dens[layer - 1, here, :] = density * ((1.0 - hardening) - growth) + hardening * saturation
            prog[layer - 1, here, :] = progress + growth

    def sweep(source, target, low, high):
        def body(layer, carry):
            update(source, target, layer)
            return carry
        lax.fori_loop(low, high, body, 0)

    def add_halo(source, middle, target, outer, inner, step, chunk):
        for row in range(chunk * part, (chunk + 1) * part, ROWS):
            here = pl.ds(PAD + row, ROWS)
            value = middle[inner, here, :] + diffusion_number * source[outer, here, :]
            middle[inner, here, :] = value
            target[inner + step, here, :] = target[inner + step, here, :] + diffusion_number * value

    def cycle(source, middle, target, parity, go):
        sweep(source, middle, 3, thick + 1)
        for inner, step in ((2, 1), (thick + 1, -1)):
            update(source, middle, inner, -step)
            update(middle, target, inner + step, -step)
        for side, inner, step in ((0, 2, 1), (1, thick + 1, -1)):
            for chunk in range(CHUNKS):
                wait_halo(source, parity, side, 0, chunk)
                add_halo(source, middle, target, inner - step, inner, step, chunk)
                send_halo(target, 1 - parity, side, 1, chunk, go)
        for side, inner, step in ((0, 2, 1), (1, thick + 1, -1)):
            @pl.when((has_low, has_high)[side])
            def _(inner=inner, step=step):
                update(source, middle, inner - step, -step)
            update(middle, target, inner, -step)
            for chunk in range(CHUNKS):
                @pl.when((has_low, has_high)[side])
                def _(side=side, inner=inner, step=step, chunk=chunk):
                    wait_halo(source, parity, side, 1, chunk)
                    add_halo(source, middle, target, inner - 2 * step, inner - step, step, chunk)
                send_halo(target, 1 - parity, side, 0, chunk, go)
        sweep(middle, target, 4, thick)
        sweep(middle, None, jnp.where(has_low, 1, 2), 2)
        sweep(middle, None, thick + 2, jnp.where(has_high, thick + 3, thick + 2))

    total = 2 * M // 4

    def four_steps(index, carry):
        cycle(heat_a, heat_b, heat_c, 0, True)
        cycle(heat_c, heat_b, heat_a, 1, index < total - 1)
        return carry

    lax.fori_loop(0, total // 2, four_steps, 0)

    def state(field, layer):
        if field == 0:
            return heat_a[layer + 2, rows, :]
        return (dens, prog)[field - 1][layer + 1]

    def keep(layer, carry):
        for field in range(3):
            relaxed[half, field, layer] = state(field, offset + layer)

        @pl.when(later)
        def _():
            for field in range(3):
                relaxed_out[field, layer] = state(field, other * depth + layer)
        return carry

    lax.fori_loop(0, depth, keep, 0)

    def relaxed_copy(chain):
        return pltpu.make_async_remote_copy(
            relaxed_out, relaxed.at[chain], relaxed_send, relaxed_recv,
            device_id=place(partner, t), device_id_type=MESH)

    def fine_copy(field, chain, where, layer):
        start = where * depth + layer
        source = heat_a.at[start + 2, rows, :] if field == 0 else (dens, prog)[field - 1].at[start + 1]
        return pltpu.make_async_remote_copy(
            source, fine.at[chain, field, layer], back_send.at[field, layer], back_recv.at[field, layer],
            device_id=place(partner, t), device_id_type=MESH)

    @pl.when(later)
    def _():
        relaxed_copy(half).start()

    lax.fori_loop(total // 2, total, four_steps, 0)

    @pl.when(later)
    def _():
        for layer in range(depth):
            for field in range(3):
                fine_copy(field, half, other, layer).start()

    def keep_fine(layer, carry):
        for field in range(3):
            fine[half, field, layer] = state(field, offset + layer)
        return carry

    lax.fori_loop(0, depth, keep_fine, 0)
    map_copy.wait()

    wait_sent(later)

    @pl.when(first)
    def _():
        for field in range(3):
            for piece in range(2):
                first_copy(half, field, piece).wait_send()

    @pl.when(later)
    def _():
        relaxed_copy(half).wait_send()
        relaxed_copy(other).wait_recv()

    def chain_copy(layer, tm):
        return pltpu.make_async_remote_copy(
            out.at[1, :, layer], arriving.at[:, layer], chain_send.at[layer], chain_recv.at[layer],
            device_id=place(s, tm), device_id_type=MESH)

    def link(layer, carry):
        @pl.when(first)
        def _():
            for field in range(3):
                out[0, field, layer] = relaxed[half, field, layer]
                out[1, field, layer] = fine[half, field, layer]

        @pl.when(later)
        def _():
            for field in range(3):
                fine_copy(field, other, half, layer).wait_recv()
            chain_copy(layer, t).wait_recv()
            for row in range(0, ny, ROWS):
                here = pl.ds(row, ROWS)
                value = [arriving[field, layer, here, :] for field in range(3)]
                for slot in range(2):
                    change = [value[field] - relaxed[slot, field, layer, here, :] for field in range(3)]
                    value = [
                        fine[slot, r, layer, here, :]
                        + (maps[r, 0, layer, here, :] * change[0] + maps[r, 1, layer, here, :] * change[1]
                           + maps[r, 2, layer, here, :] * change[2])
                        for r in range(3)
                    ]
                    for field in range(3):
                        out[slot, field, layer, here, :] = value[field]

        @pl.when(jnp.logical_not(last))
        def _():
            chain_copy(layer, t + 1).start()
        return carry

    lax.fori_loop(0, depth, link, 0)

    @pl.when(jnp.logical_not(last))
    def _():
        for layer in range(depth):
            chain_copy(layer, t + 1).wait_send()

    @pl.when(later)
    def _():
        for layer in range(depth):
            for field in range(3):
                fine_copy(field, half, other, layer).wait_send()


def shards(spaces, blocks, initial, guess, coarse_map, sites, mobility):
    depth, ny, nx = sites.shape
    thick = 2 * depth
    heat = pltpu.VMEM((thick + 4, ny + 2 * PAD, nx), jnp.float32)
    wide = pltpu.VMEM((thick + 2, ny, nx), jnp.float32)
    both = pltpu.VMEM((2, 3, depth, ny, nx), jnp.float32)
    one = pltpu.VMEM((3, depth, ny, nx), jnp.float32)
    dma = pltpu.SemaphoreType.DMA
    vmem = pl.BlockSpec(memory_space=pltpu.VMEM)
    hbm = pl.BlockSpec(memory_space=pl.ANY)
    return pl.pallas_call(
        functools.partial(kernel, spaces, blocks),
        out_shape=jax.ShapeDtypeStruct(guess.shape, jnp.float32),
        in_specs=[hbm, hbm, hbm, vmem, vmem],
        out_specs=vmem,
        scratch_shapes=[
            heat, heat, heat, wide, wide, wide, pltpu.VMEM((depth, ny, nx), jnp.float32),
            both, one, both, one, pltpu.VMEM(coarse_map.shape, jnp.float32),
            dma((2, 3, 2)), dma((2, 3, 2)), dma((3,)), dma((3, 2)), dma, dma,
            dma((2, 2, 2, CHUNKS)), dma((2, 2, 2, CHUNKS)), dma((3, 2)), dma((3, 2)),
            dma, dma, dma((3, depth)), dma((3, depth)), dma((depth,)), dma((depth,)), dma,
        ],
        compiler_params=pltpu.CompilerParams(
            collective_id=0, has_side_effects=True, vmem_limit_bytes=60 * 1024 * 1024),
    )(initial, guess, coarse_map, sites, mobility.reshape(1, -1))


def solution(mesh):
    placed = (
        P(None, "space", None, None),
        P("tm", None, "space", None, None),
        P(None, None, "space", None, None),
        P("space", None, None),
        P(),
    )
    return jax.shard_map(
        functools.partial(shards, mesh.shape["space"], mesh.shape["tm"]),
        mesh=mesh,
        in_specs=placed,
        out_specs=P("tm", None, "space", None, None),
        check_vma=False,
    )
```

```python
import functools

import jax
import jax.numpy as jnp
from jax import lax
from jax.experimental import pallas as pl
from jax.experimental.pallas import tpu as pltpu
from jax.sharding import PartitionSpec as P

M = 16
PAD = 8
ROWS = 32
EDGE = 2
CHUNKS = 4
MESH = pl.DeviceIdType.MESH

diffusion_number = 0.15
heat_release = 0.5
hardening = 0.02
saturation = 2.0


def kernel(
    spaces, blocks,
    initial, guess, coarse, sites, mobility, out,
    heat_a, heat_b, heat_c, dens, prog, mobile, own_mobile,
    relaxed, relaxed_out, fine, arriving, maps,
    start_send, start_recv, local_sem, first_send, mob_send, mob_recv,
    halo_send, halo_recv, edge_send, edge_recv,
    relaxed_send, relaxed_recv, back_send, back_recv, chain_send, chain_recv, map_sem,
):
    depth = sites.shape[0]
    ny, nx = sites.shape[1], sites.shape[2]
    s, t = lax.axis_index("space"), lax.axis_index("tm")
    half = lax.rem(s, 2)
    first, last = t == 0, t == blocks - 1
    later = jnp.logical_not(first)
    thick, stride = 2 * depth, 2
    offset = half * depth
    other = 1 - half
    base = s - half
    partner = base + other
    has_low, has_high = s >= stride, s < spaces - stride
    rows = pl.ds(PAD, ny)

    barrier = pltpu.get_barrier_semaphore()

    def place(space, tm):
        return {"space": space, "tm": tm}

    zero_rows = jnp.zeros((PAD, nx), jnp.float32)
    for heat in (heat_a, heat_b, heat_c):
        for layer in range(2 * depth + 4):
            heat[layer, pl.ds(0, PAD), :] = zero_rows
            heat[layer, pl.ds(PAD + ny, PAD), :] = zero_rows
        for layer in (0, 1, thick + 2, thick + 3):
            heat[layer, rows, :] = jnp.zeros((ny, nx), jnp.float32)

    friends = [
        (t >= 0, partner, t),
        (t > 0, base, t - 1), (t > 0, base + 1, t - 1),
        (t < blocks - 1, base, t + 1), (t < blocks - 1, base + 1, t + 1),
        (has_low, s - stride, t), (has_high, s + stride, t),
    ]
    count = 0
    for there, layer in ((has_low, 0), (has_high, thick + 1)):
        @pl.when(jnp.logical_not(there))
        def _(layer=layer):
            for ref in (dens, prog, mobile):
                ref[layer] = jnp.zeros((ny, nx), jnp.float32)

    for there, space, tm in friends:
        @pl.when(there)
        def _(space=space, tm=tm):
            pl.semaphore_signal(barrier, 1, device_id=place(space, tm), device_id_type=MESH)
        count = count + there.astype(jnp.int32)
    def piece_of(source, piece):
        if piece == 0:
            return source * (depth - EDGE), EDGE
        return (1 - source) * EDGE, depth - EDGE

    def landing(field, where, low, layers):
        start = where * depth + low
        if field == 0:
            return heat_a.at[pl.ds(start + 2, layers), rows, :]
        return (dens, prog)[field - 1].at[pl.ds(start + 1, layers)]

    def start_copy(source, chain, field, piece, tm):
        low, layers = piece_of(source, piece)
        return pltpu.make_async_remote_copy(
            guess.at[chain, field, pl.ds(low, layers)], landing(field, source, low, layers),
            start_send.at[chain, field, piece], start_recv.at[source, field, piece],
            device_id=place(base + chain, tm), device_id_type=MESH)

    def local_copy(field):
        return pltpu.make_async_copy(initial.at[field], landing(field, half, 0, depth), local_sem.at[field])

    def first_copy(source, field, piece):
        low, layers = piece_of(source, piece)
        return pltpu.make_async_remote_copy(
            initial.at[field, pl.ds(low, layers)], landing(field, source, low, layers),
            first_send.at[field, piece], start_recv.at[source, field, piece],
            device_id=place(partner, t), device_id_type=MESH)

    map_copy = pltpu.make_async_copy(coarse, maps, map_sem)

    @pl.when(first)
    def _():
        for field in range(3):
            local_copy(field).start()

    table = jnp.broadcast_to(mobility[...], (8, nx))

    def look_up(layer, carry):
        for row in range(0, ny, 8):
            index = sites[layer, pl.ds(row, 8), :]
            found = jnp.take_along_axis(table, index, axis=1, mode="promise_in_bounds")
            own_mobile[layer, pl.ds(row, 8), :] = found
            mobile[layer + 1 + offset, pl.ds(row, 8), :] = found
        return carry

    lax.fori_loop(0, depth, look_up, 0)
    quarter = depth // 2
    share = lax.rem(t, 2)

    def mobile_copy():
        return pltpu.make_async_remote_copy(
            own_mobile.at[pl.ds(share * quarter, quarter)],
            mobile.at[pl.ds(1 + half * depth + share * quarter, quarter)], mob_send.at[0], mob_recv.at[0],
            device_id=place(partner, t), device_id_type=MESH)

    def mobile_pass(which):
        some = mobile.at[pl.ds(1 + other * depth + which * quarter, quarter)]
        return pltpu.make_async_remote_copy(
            some, some, mob_send.at[1], mob_recv.at[1],
            device_id=place(s, t + 1 - 2 * share), device_id_type=MESH)

    pl.semaphore_wait(barrier, count)

    odd = lax.rem(t, 2) == 1
    deferred = jnp.logical_and(later, jnp.logical_not(odd))

    def send_start(go):
        @pl.when(jnp.logical_and(jnp.logical_not(last), go))
        def _():
            for piece in range(2):
                for field in range(3):
                    for chain in range(2):
                        start_copy(half, chain, field, piece, t + 1).start()

    def wait_sent(pieces, go):
        @pl.when(jnp.logical_and(jnp.logical_not(last), go))
        def _():
            for field in range(3):
                for chain in range(2):
                    for piece in pieces:
                        start_copy(half, chain, field, piece, t + 1).wait_send()

    def wait_start(piece):
        for field in range(3):
            start_copy(other, 0, field, piece, t).wait_recv()

        @pl.when(later)
        def _():
            for field in range(3):
                start_copy(half, 0, field, piece, t).wait_recv()

    send_start(jnp.logical_not(deferred))

    mobile_copy().start()
    map_copy.start()
    wait_sent((0,), first)

    @pl.when(first)
    def _():
        for piece in range(2):
            for field in range(3):
                first_copy(half, field, piece).start()
        for field in range(3):
            local_copy(field).wait()

    wait_start(0)

    part = ny // CHUNKS

    def halo(heat, parity, side, far, chunk):
        source, target, space = (
            (2 + far, thick + 2 + far, s - stride), (thick + 1 - far, 1 - far, s + stride))[side]
        some = pl.ds(PAD + chunk * part, part)
        return pltpu.make_async_remote_copy(
            heat.at[source, some, :], heat.at[target, some, :],
            halo_send.at[parity, side, far, chunk], halo_recv.at[parity, side, far, chunk],
            device_id=place(space, t), device_id_type=MESH)

    def send_halo(heat, parity, side, far, chunk, go):
        @pl.when(jnp.logical_and((has_low, has_high)[side], go))
        def _():
            halo(heat, parity, side, far, chunk).start()

    def wait_halo(heat, parity, side, far, chunk):
        @pl.when((has_low, has_high)[side])
        def _():
            halo(heat, parity, side, far, chunk).wait_send()
            halo(heat, parity, 1 - side, far, chunk).wait_recv()

    for far in range(2):
        for side in range(2):
            for chunk in range(CHUNKS):
                send_halo(heat_a, 0, side, far, chunk, True)
    edges = (dens, prog, mobile)

    def edge(number, side):
        ref = edges[number]
        source, target, space = ((1, thick + 1, s - stride), (thick, 0, s + stride))[side]
        return pltpu.make_async_remote_copy(
            ref.at[source], ref.at[target], edge_send.at[number, side], edge_recv.at[number, side],
            device_id=place(space, t), device_id_type=MESH)

    def send_edges(numbers):
        for side in range(2):
            @pl.when((has_low, has_high)[side])
            def _(side=side):
                for number in numbers:
                    edge(number, side).start()

    send_edges((0, 1))
    send_start(deferred)

    mobile_copy().wait()
    mobile_pass(share).start()
    mobile_pass(1 - share).wait_recv()

    send_edges((2,))

    wait_start(1)

    for side in range(2):
        @pl.when((has_low, has_high)[side])
        def _(side=side):
            for number in range(3):
                edge(number, side).wait_send()
                edge(number, 1 - side).wait_recv()

    lane = lax.broadcasted_iota(jnp.int32, (ROWS, nx), 1)
    not_first, not_last = lane > 0, lane < nx - 1

    def update(source, target, layer, skip=0):
        for row in range(0, ny, ROWS):
            here = pl.ds(row, ROWS)
            center = source[layer, pl.ds(PAD + row, ROWS), :]
            density = dens[layer - 1, here, :]
            progress = prog[layer - 1, here, :]
            square = density * density
            driving = square * pl.reciprocal(1.0 + square)
            growth = mobile[layer - 1, here, :] * (1.0 + 0.5 * jnp.tanh(center)) * driving
            growth = growth * (1.0 - jnp.tanh(progress))
            if target is not None:
                around = source[layer, pl.ds(PAD + row - 1, ROWS), :] + source[layer, pl.ds(PAD + row + 1, ROWS), :]
                if skip != -1:
                    around = around + source[layer - 1, pl.ds(PAD + row, ROWS), :]
                if skip != 1:
                    around = around + source[layer + 1, pl.ds(PAD + row, ROWS), :]
                left = jnp.where(not_first, pltpu.roll(center, 1, 1), 0.0)
                right = jnp.where(not_last, pltpu.roll(center, nx - 1, 1), 0.0)
                around = around + (left + right)
                target[layer, pl.ds(PAD + row, ROWS), :] = (
                    (1.0 - 6.0 * diffusion_number) * center + diffusion_number * around + heat_release * growth)
            dens[layer - 1, here, :] = density * ((1.0 - hardening) - growth) + hardening * saturation
            prog[layer - 1, here, :] = progress + growth

    def add_halo(source, middle, target, outer, inner, step, chunk):
        for row in range(chunk * part, (chunk + 1) * part, ROWS):
            here = pl.ds(PAD + row, ROWS)
            value = middle[inner, here, :] + diffusion_number * source[outer, here, :]
            middle[inner, here, :] = value
            target[inner + step, here, :] = target[inner + step, here, :] + diffusion_number * value

    ends = ((0, 2, 1), (1, thick + 1, -1))

    def fine_copy(field, chain, where, layer):
        start = where * depth + layer
        source = heat_a.at[start + 2, rows, :] if field == 0 else (dens, prog)[field - 1].at[start + 1]
        return pltpu.make_async_remote_copy(
            source, fine.at[chain, field, layer], back_send.at[field, layer], back_recv.at[field, layer],
            device_id=place(partner, t), device_id_type=MESH)

    def send_fine(piece):
        low, layers = piece_of(other, piece)
        for layer in range(layers):
            for field in range(3):
                fine_copy(field, half, other, low + layer).start()

    def cycle(source, middle, target, parity, order, go):
        for layer in range(3, thick + 1):
            update(source, middle, layer)
        for _, inner, step in order:
            update(source, middle, inner, -step)
        for layer in range(4, thick):
            update(middle, target, layer)
        for _, inner, step in order:
            update(middle, target, inner + step, -step)
        if go is not True:
            @pl.when(jnp.logical_and(jnp.logical_not(go), later))
            def _():
                send_fine(1)
        for side, inner, step in order:
            for chunk in range(CHUNKS):
                wait_halo(source, parity, side, 0, chunk)
                add_halo(source, middle, target, inner - step, inner, step, chunk)
                send_halo(target, 1 - parity, side, 1, chunk, go)
            update(source, middle, inner - step, -step)
            update(middle, target, inner, -step)
            for chunk in range(CHUNKS):
                @pl.when((has_low, has_high)[side])
                def _(side=side, inner=inner, step=step, chunk=chunk):
                    wait_halo(source, parity, side, 1, chunk)
                    add_halo(source, middle, target, inner - 2 * step, inner - step, step, chunk)
                send_halo(target, 1 - parity, side, 0, chunk, go)
        for _, inner, step in order:
            update(middle, None, inner - step)

    total = 2 * M // 4

    def state(field, layer):
        if field == 0:
            return heat_a[layer + 2, rows, :]
        return (dens, prog)[field - 1][layer + 1]

    def keep(layer, carry):
        for field in range(3):
            relaxed[half, field, layer] = state(field, offset + layer)

        @pl.when(later)
        def _():
            for field in range(3):
                relaxed_out[field, layer] = state(field, other * depth + layer)
        return carry

    def relaxed_copy(chain):
        return pltpu.make_async_remote_copy(
            relaxed_out, relaxed.at[chain], relaxed_send, relaxed_recv,
            device_id=place(partner, t), device_id_type=MESH)

    def four_steps(index, carry):
        @pl.when(index == total // 2)
        def _():
            lax.fori_loop(0, depth, keep, 0)

            @pl.when(later)
            def _():
                relaxed_copy(half).start()

        cycle(heat_a, heat_b, heat_c, 0, ends, True)
        cycle(heat_c, heat_b, heat_a, 1, ends[::-1], index < total - 1)
        return carry

    lax.fori_loop(0, total, four_steps, 0)

    @pl.when(later)
    def _():
        send_fine(0)

    def keep_fine(layer, carry):
        for field in range(3):
            fine[half, field, layer] = state(field, offset + layer)
        return carry

    lax.fori_loop(0, depth, keep_fine, 0)
    map_copy.wait()

    wait_sent((0,), later)
    wait_sent((1,), True)
    mobile_pass(share).wait_send()

    @pl.when(first)
    def _():
        for field in range(3):
            for piece in range(2):
                first_copy(half, field, piece).wait_send()

    @pl.when(later)
    def _():
        relaxed_copy(half).wait_send()
        relaxed_copy(other).wait_recv()

    def chain_copy(layer, tm):
        return pltpu.make_async_remote_copy(
            out.at[1, :, layer], arriving.at[:, layer], chain_send.at[layer], chain_recv.at[layer],
            device_id=place(s, tm), device_id_type=MESH)

    def link(index, carry):
        layer = lax.rem(index + other * EDGE, depth)

        @pl.when(first)
        def _():
            for field in range(3):
                out[0, field, layer] = relaxed[half, field, layer]
                out[1, field, layer] = fine[half, field, layer]

        @pl.when(later)
        def _():
            for field in range(3):
                fine_copy(field, other, half, layer).wait_recv()
            chain_copy(layer, t).wait_recv()
            for row in range(0, ny, ROWS):
                here = pl.ds(row, ROWS)
                value = [arriving[field, layer, here, :] for field in range(3)]
                for slot in range(2):
                    change = [value[field] - relaxed[slot, field, layer, here, :] for field in range(3)]
                    value = [
                        fine[slot, r, layer, here, :]
                        + (maps[r, 0, layer, here, :] * change[0] + maps[r, 1, layer, here, :] * change[1]
                           + maps[r, 2, layer, here, :] * change[2])
                        for r in range(3)
                    ]
                    for field in range(3):
                        out[slot, field, layer, here, :] = value[field]

        @pl.when(jnp.logical_not(last))
        def _():
            chain_copy(layer, t + 1).start()
        return carry

    lax.fori_loop(0, depth, link, 0)

    @pl.when(jnp.logical_not(last))
    def _():
        for layer in range(depth):
            chain_copy(layer, t + 1).wait_send()

    @pl.when(later)
    def _():
        for layer in range(depth):
            for field in range(3):
                fine_copy(field, half, other, layer).wait_send()


def shards(spaces, blocks, initial, guess, coarse_map, sites, mobility):
    depth, ny, nx = sites.shape
    thick = 2 * depth
    heat = pltpu.VMEM((thick + 4, ny + 2 * PAD, nx), jnp.float32)
    wide = pltpu.VMEM((thick + 2, ny, nx), jnp.float32)
    both = pltpu.VMEM((2, 3, depth, ny, nx), jnp.float32)
    one = pltpu.VMEM((3, depth, ny, nx), jnp.float32)
    dma = pltpu.SemaphoreType.DMA
    vmem = pl.BlockSpec(memory_space=pltpu.VMEM)
    hbm = pl.BlockSpec(memory_space=pl.ANY)
    return pl.pallas_call(
        functools.partial(kernel, spaces, blocks),
        out_shape=jax.ShapeDtypeStruct(guess.shape, jnp.float32),
        in_specs=[hbm, hbm, hbm, vmem, vmem],
        out_specs=vmem,
        scratch_shapes=[
            heat, heat, heat, wide, wide, wide, pltpu.VMEM((depth, ny, nx), jnp.float32),
            both, one, both, one, pltpu.VMEM(coarse_map.shape, jnp.float32),
            dma((2, 3, 2)), dma((2, 3, 2)), dma((3,)), dma((3, 2)), dma((2,)), dma((2,)),
            dma((2, 2, 2, CHUNKS)), dma((2, 2, 2, CHUNKS)), dma((3, 2)), dma((3, 2)),
            dma, dma, dma((3, depth)), dma((3, depth)), dma((depth,)), dma((depth,)), dma,
        ],
        compiler_params=pltpu.CompilerParams(
            collective_id=0, has_side_effects=True, vmem_limit_bytes=60 * 1024 * 1024),
    )(initial, guess, coarse_map, sites, mobility.reshape(1, -1))


def solution(mesh):
    placed = (
        P(None, "space", None, None),
        P("tm", None, "space", None, None),
        P(None, None, "space", None, None),
        P("space", None, None),
        P(),
    )
    return jax.shard_map(
        functools.partial(shards, mesh.shape["space"], mesh.shape["tm"]),
        mesh=mesh,
        in_specs=placed,
        out_specs=P("tm", None, "space", None, None),
        check_vma=False,
    )
```

```python
import functools

import jax
import jax.numpy as jnp
from jax import lax
from jax.experimental import pallas as pl
from jax.experimental.pallas import tpu as pltpu
from jax.sharding import PartitionSpec as P

M = 16
PAD = 8
ROWS = 32
EDGE = 2
CHUNKS = 4
MESH = pl.DeviceIdType.MESH

diffusion_number = 0.15
heat_release = 0.5
hardening = 0.02
saturation = 2.0


def kernel(
    spaces, blocks,
    initial, guess, coarse, sites, mobility, out,
    heat_a, heat_b, heat_c, dens, prog, mobile, own_mobile,
    relaxed, relaxed_out, fine, arriving, maps,
    start_send, start_recv, local_sem, first_send, mob_send, mob_recv,
    halo_send, halo_recv, edge_send, edge_recv,
    relaxed_send, relaxed_recv, back_send, back_recv, chain_send, chain_recv, map_sem,
):
    depth = sites.shape[0]
    ny, nx = sites.shape[1], sites.shape[2]
    s, t = lax.axis_index("space"), lax.axis_index("tm")
    half = lax.rem(s, 2)
    first, last = t == 0, t == blocks - 1
    later = jnp.logical_not(first)
    share = lax.rem(t, 2)
    odd = share == 1
    mate = t + 1 - 2 * share
    opening = t == 1
    distant = jnp.logical_and(odd, t > 2)
    near = jnp.logical_not(distant)
    sender = jnp.logical_and(odd, t + 2 < blocks)
    both_ways = jnp.logical_not(opening)
    thick, stride = 2 * depth, 2
    offset = half * depth
    other = 1 - half
    base = s - half
    partner = base + other
    has_low, has_high = s >= stride, s < spaces - stride
    rows = pl.ds(PAD, ny)

    barrier = pltpu.get_barrier_semaphore()

    def place(space, tm):
        return {"space": space, "tm": tm}

    zero_rows = jnp.zeros((PAD, nx), jnp.float32)
    for heat in (heat_a, heat_b, heat_c):
        for layer in range(2 * depth + 4):
            heat[layer, pl.ds(0, PAD), :] = zero_rows
            heat[layer, pl.ds(PAD + ny, PAD), :] = zero_rows
        for layer in (0, 1, thick + 2, thick + 3):
            heat[layer, rows, :] = jnp.zeros((ny, nx), jnp.float32)

    friends = [
        (t >= 0, partner, t), (t >= 0, s, mate), (t >= 0, partner, mate),
        (distant, base, t - 2), (distant, base + 1, t - 2),
        (sender, base, t + 2), (sender, base + 1, t + 2),
        (jnp.logical_and(odd, t + 1 < blocks), s, t + 1),
        (jnp.logical_and(jnp.logical_not(odd), t > 0), s, t - 1),
        (has_low, s - stride, t), (has_high, s + stride, t),
    ]
    count = 0
    for there, layer in ((has_low, 0), (has_high, thick + 1)):
        @pl.when(jnp.logical_not(there))
        def _(layer=layer):
            for ref in (dens, prog, mobile):
                ref[layer] = jnp.zeros((ny, nx), jnp.float32)

    for there, space, tm in friends:
        @pl.when(there)
        def _(space=space, tm=tm):
            pl.semaphore_signal(barrier, 1, device_id=place(space, tm), device_id_type=MESH)
        count = count + there.astype(jnp.int32)

    def piece_of(source, piece):
        if piece == 0:
            return source * (depth - EDGE), EDGE
        return (1 - source) * EDGE, depth - EDGE

    def landing(field, where, low, layers):
        start = where * depth + low
        if field == 0:
            return heat_a.at[pl.ds(start + 2, layers), rows, :]
        return (dens, prog)[field - 1].at[pl.ds(start + 1, layers)]

    def start_copy(source, chain, field, piece, tm):
        low, layers = piece_of(source, piece)
        return pltpu.make_async_remote_copy(
            guess.at[chain, field, pl.ds(low, layers)], landing(field, source, low, layers),
            start_send.at[chain, field, piece], start_recv.at[source, field, piece],
            device_id=place(base + chain, tm), device_id_type=MESH)

    def own_start(field, low, layers, mine):
        some = pl.ds(low, layers)
        return guess.at[half if mine else other, field, some], initial.at[field, some]

    def local_copy(field, source):
        return pltpu.make_async_copy(
            own_start(field, 0, depth, True)[source], landing(field, half, 0, depth), local_sem.at[field])

    def swap_copy(field, piece, source):
        low, layers = piece_of(half, piece)
        return pltpu.make_async_remote_copy(
            own_start(field, low, layers, False)[source], landing(field, half, low, layers),
            first_send.at[field, piece], start_recv.at[half, field, piece],
            device_id=place(partner, t), device_id_type=MESH)

    def send_swap(source):
        for piece in range(2):
            for field in range(3):
                swap_copy(field, piece, source).start()

    map_copy = pltpu.make_async_copy(coarse, maps, map_sem)

    @pl.when(jnp.logical_not(odd))
    def _():
        for field in range(3):
            local_copy(field, 0).start()

    @pl.when(opening)
    def _():
        for field in range(3):
            local_copy(field, 1).start()

    table = jnp.broadcast_to(mobility[...], (8, nx))

    def look_up(layer, carry):
        for row in range(0, ny, 8):
            index = sites[layer, pl.ds(row, 8), :]
            found = jnp.take_along_axis(table, index, axis=1, mode="promise_in_bounds")
            own_mobile[layer, pl.ds(row, 8), :] = found
            mobile[layer + 1 + offset, pl.ds(row, 8), :] = found
        return carry

    lax.fori_loop(0, depth, look_up, 0)
    quarter = depth // 2

    def mobile_copy():
        return pltpu.make_async_remote_copy(
            own_mobile.at[pl.ds(share * quarter, quarter)],
            mobile.at[pl.ds(1 + half * depth + share * quarter, quarter)], mob_send.at[0], mob_recv.at[0],
            device_id=place(partner, t), device_id_type=MESH)

    def mobile_pass(which):
        some = mobile.at[pl.ds(1 + other * depth + which * quarter, quarter)]
        return pltpu.make_async_remote_copy(
            some, some, mob_send.at[1], mob_recv.at[1],
            device_id=place(s, mate), device_id_type=MESH)

    pl.semaphore_wait(barrier, count)

    def wait_sent(pieces):
        @pl.when(sender)
        def _():
            for field in range(3):
                for chain in range(2):
                    for piece in pieces:
                        start_copy(half, chain, field, piece, t + 2).wait_send()

    def wait_start(piece):
        for field in range(3):
            start_copy(other, 0, field, piece, t).wait_recv()

        @pl.when(distant)
        def _():
            for field in range(3):
                start_copy(half, 0, field, piece, t).wait_recv()

    mobile_copy().start()

    @pl.when(jnp.logical_not(odd))
    def _():
        send_swap(0)

    @pl.when(sender)
    def _():
        for piece in range(2):
            for field in range(3):
                for chain in range(2):
                    start_copy(half, chain, field, piece, t + 2).start()

    mobile_copy().wait()
    mobile_pass(share).start()
    map_copy.start()
    wait_sent((0,))

    @pl.when(opening)
    def _():
        send_swap(1)

    @pl.when(near)
    def _():
        for field in range(3):
            local_copy(field, 0).wait()

    wait_start(0)

    part = ny // CHUNKS

    def halo(heat, parity, side, far, chunk):
        source, target, space = (
            (2 + far, thick + 2 + far, s - stride), (thick + 1 - far, 1 - far, s + stride))[side]
        some = pl.ds(PAD + chunk * part, part)
        return pltpu.make_async_remote_copy(
            heat.at[source, some, :], heat.at[target, some, :],
            halo_send.at[parity, side, far, chunk], halo_recv.at[parity, side, far, chunk],
            device_id=place(space, t), device_id_type=MESH)

    def send_halo(heat, parity, side, far, chunk, go):
        @pl.when(jnp.logical_and((has_low, has_high)[side], go))
        def _():
            halo(heat, parity, side, far, chunk).start()

    def wait_halo(heat, parity, side, far, chunk):
        @pl.when((has_low, has_high)[side])
        def _():
            halo(heat, parity, side, far, chunk).wait_send()
            halo(heat, parity, 1 - side, far, chunk).wait_recv()

    for far in range(2):
        for side in range(2):
            for chunk in range(CHUNKS):
                send_halo(heat_a, 0, side, far, chunk, True)
    edges = (dens, prog, mobile)

    def edge(number, side):
        ref = edges[number]
        source, target, space = ((1, thick + 1, s - stride), (thick, 0, s + stride))[side]
        return pltpu.make_async_remote_copy(
            ref.at[source], ref.at[target], edge_send.at[number, side], edge_recv.at[number, side],
            device_id=place(space, t), device_id_type=MESH)

    def send_edges(numbers):
        for side in range(2):
            @pl.when((has_low, has_high)[side])
            def _(side=side):
                for number in numbers:
                    edge(number, side).start()

    send_edges((0, 1))

    mobile_pass(1 - share).wait_recv()

    send_edges((2,))

    wait_start(1)

    for side in range(2):
        @pl.when((has_low, has_high)[side])
        def _(side=side):
            for number in range(3):
                edge(number, side).wait_send()
                edge(number, 1 - side).wait_recv()

    lane = lax.broadcasted_iota(jnp.int32, (ROWS, nx), 1)
    not_first, not_last = lane > 0, lane < nx - 1

    def update(source, target, layer, skip=0):
        for row in range(0, ny, ROWS):
            here = pl.ds(row, ROWS)
            center = source[layer, pl.ds(PAD + row, ROWS), :]
            density = dens[layer - 1, here, :]
            progress = prog[layer - 1, here, :]
            square = density * density
            driving = square * pl.reciprocal(1.0 + square)
            growth = mobile[layer - 1, here, :] * (1.0 + 0.5 * jnp.tanh(center)) * driving
            growth = growth * (1.0 - jnp.tanh(progress))
            if target is not None:
                around = source[layer, pl.ds(PAD + row - 1, ROWS), :] + source[layer, pl.ds(PAD + row + 1, ROWS), :]
                if skip != -1:
                    around = around + source[layer - 1, pl.ds(PAD + row, ROWS), :]
                if skip != 1:
                    around = around + source[layer + 1, pl.ds(PAD + row, ROWS), :]
                left = jnp.where(not_first, pltpu.roll(center, 1, 1), 0.0)
                right = jnp.where(not_last, pltpu.roll(center, nx - 1, 1), 0.0)
                around = around + (left + right)
                target[layer, pl.ds(PAD + row, ROWS), :] = (
                    (1.0 - 6.0 * diffusion_number) * center + diffusion_number * around + heat_release * growth)
            dens[layer - 1, here, :] = density * ((1.0 - hardening) - growth) + hardening * saturation
            prog[layer - 1, here, :] = progress + growth

    def add_halo(source, middle, target, outer, inner, step, chunk):
        for row in range(chunk * part, (chunk + 1) * part, ROWS):
            here = pl.ds(PAD + row, ROWS)
            value = middle[inner, here, :] + diffusion_number * source[outer, here, :]
            middle[inner, here, :] = value
            target[inner + step, here, :] = target[inner + step, here, :] + diffusion_number * value

    ends = ((0, 2, 1), (1, thick + 1, -1))

    def fine_copy(field, where, layer, slot):
        start = where * depth + layer
        source = heat_a.at[start + 2, rows, :] if field == 0 else (dens, prog)[field - 1].at[start + 1]
        return pltpu.make_async_remote_copy(
            source, fine.at[slot, field, layer], back_send.at[where, field, layer], back_recv.at[slot, field, layer],
            device_id=place(base + where, mate), device_id_type=MESH)

    def send_fine(piece):
        def send(where):
            low, layers = piece_of(where, piece)
            for layer in range(layers):
                for field in range(3):
                    fine_copy(field, where, low + layer, half).start()

        @pl.when(both_ways)
        def _():
            send(other)
        send(half)

    def cycle(source, middle, target, parity, order, go):
        for layer in range(3, thick + 1):
            update(source, middle, layer)
        for _, inner, step in order:
            update(source, middle, inner, -step)
        for layer in range(4, thick):
            update(middle, target, layer)
        for _, inner, step in order:
            update(middle, target, inner + step, -step)
        if go is not True:
            @pl.when(jnp.logical_not(go))
            def _():
                send_fine(1)
        for side, inner, step in order:
            for chunk in range(CHUNKS):
                wait_halo(source, parity, side, 0, chunk)
                add_halo(source, middle, target, inner - step, inner, step, chunk)
                send_halo(target, 1 - parity, side, 1, chunk, go)
            update(source, middle, inner - step, -step)
            update(middle, target, inner, -step)
            for chunk in range(CHUNKS):
                @pl.when((has_low, has_high)[side])
                def _(side=side, inner=inner, step=step, chunk=chunk):
                    wait_halo(source, parity, side, 1, chunk)
                    add_halo(source, middle, target, inner - 2 * step, inner - step, step, chunk)
                send_halo(target, 1 - parity, side, 0, chunk, go)
        for _, inner, step in order:
            update(middle, None, inner - step)

    total = 2 * M // 4

    def state(field, layer):
        if field == 0:
            return heat_a[layer + 2, rows, :]
        return (dens, prog)[field - 1][layer + 1]

    def keep(layer, carry):
        for where in range(2):
            for field in range(3):
                relaxed_out[where, field, layer] = state(field, where * depth + layer)
        return carry

    def relaxed_copy(where, slot):
        return pltpu.make_async_remote_copy(
            relaxed_out.at[where], relaxed.at[slot], relaxed_send.at[where], relaxed_recv.at[slot],
            device_id=place(base + where, mate), device_id_type=MESH)

    def four_steps(index, carry):
        @pl.when(index == total // 2)
        def _():
            lax.fori_loop(0, depth, keep, 0)
            relaxed_copy(half, half).start()

            @pl.when(both_ways)
            def _():
                relaxed_copy(other, half).start()

        cycle(heat_a, heat_b, heat_c, 0, ends, True)
        cycle(heat_c, heat_b, heat_a, 1, ends[::-1], index < total - 1)
        return carry

    lax.fori_loop(0, total, four_steps, 0)

    send_fine(0)
    map_copy.wait()
    wait_sent((1,))
    mobile_pass(share).wait_send()

    @pl.when(near)
    def _():
        for field in range(3):
            for piece in range(2):
                swap_copy(field, piece, 0).wait_send()

    relaxed_copy(half, half).wait_send()

    @pl.when(both_ways)
    def _():
        relaxed_copy(other, half).wait_send()

    relaxed_copy(half, half).wait_recv()

    @pl.when(later)
    def _():
        relaxed_copy(half, other).wait_recv()

    def chain_copy(layer, tm):
        return pltpu.make_async_remote_copy(
            out.at[1, :, layer], arriving.at[:, layer], chain_send.at[layer], chain_recv.at[layer],
            device_id=place(s, tm), device_id_type=MESH)

    def link(index, carry):
        layer = lax.rem(index + other * EDGE, depth)

        for field in range(3):
            fine_copy(field, half, layer, half).wait_recv()

        @pl.when(first)
        def _():
            for field in range(3):
                out[0, field, layer] = relaxed[half, field, layer]
                out[1, field, layer] = fine[half, field, layer]

        @pl.when(later)
        def _():
            for field in range(3):
                fine_copy(field, half, layer, other).wait_recv()
            chain_copy(layer, t).wait_recv()
            for row in range(0, ny, ROWS):
                here = pl.ds(row, ROWS)
                value = [arriving[field, layer, here, :] for field in range(3)]
                for slot in range(2):
                    change = [value[field] - relaxed[slot, field, layer, here, :] for field in range(3)]
                    value = [
                        fine[slot, r, layer, here, :]
                        + (maps[r, 0, layer, here, :] * change[0] + maps[r, 1, layer, here, :] * change[1]
                           + maps[r, 2, layer, here, :] * change[2])
                        for r in range(3)
                    ]
                    for field in range(3):
                        out[slot, field, layer, here, :] = value[field]

        @pl.when(jnp.logical_not(last))
        def _():
            chain_copy(layer, t + 1).start()
        return carry

    lax.fori_loop(0, depth, link, 0)

    @pl.when(jnp.logical_not(last))
    def _():
        for layer in range(depth):
            chain_copy(layer, t + 1).wait_send()

    for layer in range(depth):
        for field in range(3):
            fine_copy(field, half, layer, half).wait_send()

    @pl.when(both_ways)
    def _():
        for layer in range(depth):
            for field in range(3):
                fine_copy(field, other, layer, half).wait_send()


def shards(spaces, blocks, initial, guess, coarse_map, sites, mobility):
    depth, ny, nx = sites.shape
    thick = 2 * depth
    heat = pltpu.VMEM((thick + 4, ny + 2 * PAD, nx), jnp.float32)
    wide = pltpu.VMEM((thick + 2, ny, nx), jnp.float32)
    both = pltpu.VMEM((2, 3, depth, ny, nx), jnp.float32)
    one = pltpu.VMEM((3, depth, ny, nx), jnp.float32)
    dma = pltpu.SemaphoreType.DMA
    vmem = pl.BlockSpec(memory_space=pltpu.VMEM)
    hbm = pl.BlockSpec(memory_space=pl.ANY)
    return pl.pallas_call(
        functools.partial(kernel, spaces, blocks),
        out_shape=jax.ShapeDtypeStruct(guess.shape, jnp.float32),
        in_specs=[hbm, hbm, hbm, vmem, vmem],
        out_specs=vmem,
        scratch_shapes=[
            heat, heat, heat, wide, wide, wide, pltpu.VMEM((depth, ny, nx), jnp.float32),
            both, both, both, one, pltpu.VMEM(coarse_map.shape, jnp.float32),
            dma((2, 3, 2)), dma((2, 3, 2)), dma((3,)), dma((3, 2)), dma((2,)), dma((2,)),
            dma((2, 2, 2, CHUNKS)), dma((2, 2, 2, CHUNKS)), dma((3, 2)), dma((3, 2)),
            dma((2,)), dma((2,)), dma((2, 3, depth)), dma((2, 3, depth)), dma((depth,)), dma((depth,)), dma,
        ],
        compiler_params=pltpu.CompilerParams(
            collective_id=0, has_side_effects=True, vmem_limit_bytes=60 * 1024 * 1024),
    )(initial, guess, coarse_map, sites, mobility.reshape(1, -1))


def solution(mesh):
    placed = (
        P(None, "space", None, None),
        P("tm", None, "space", None, None),
        P(None, None, "space", None, None),
        P("space", None, None),
        P(),
    )
    return jax.shard_map(
        functools.partial(shards, mesh.shape["space"], mesh.shape["tm"]),
        mesh=mesh,
        in_specs=placed,
        out_specs=P("tm", None, "space", None, None),
        check_vma=False,
    )
```

```python
import functools

import jax
import jax.numpy as jnp
from jax import lax
from jax.experimental import pallas as pl
from jax.experimental.pallas import tpu as pltpu
from jax.sharding import PartitionSpec as P

M = 16
PAD = 8
ROWS = 32
EDGE = 2
CHUNKS = 8
SOME = 16
PARTS = 2
MESH = pl.DeviceIdType.MESH

diffusion_number = 0.15
heat_release = 0.5
hardening = 0.02
saturation = 2.0


def kernel(
    spaces, blocks,
    initial, guess, coarse, sites, mobility, result,
    heat_a, heat_b, heat_c, dens, prog, mobile, own_mobile,
    relaxed, relaxed_out, fine, out, arriving, maps,
    start_send, start_recv, local_sem, first_send, mob_send, mob_recv,
    halo_send, halo_recv, edge_send, edge_recv,
    relaxed_send, relaxed_recv, back_send, back_recv, chain_send, chain_recv, map_sem, out_sem,
):
    depth = sites.shape[0]
    ny, nx = sites.shape[1], sites.shape[2]
    s, t = lax.axis_index("space"), lax.axis_index("tm")
    half = lax.rem(s, 2)
    first, last = t == 0, t == blocks - 1
    later = jnp.logical_not(first)
    share = lax.rem(t, 2)
    odd = share == 1
    mate = t + 1 - 2 * share
    opening = t == 1
    distant = jnp.logical_and(odd, t > 2)
    near = jnp.logical_not(distant)
    sender = jnp.logical_and(odd, t + 2 < blocks)
    both_ways = jnp.logical_not(opening)
    thick, stride = 2 * depth, 2
    offset = half * depth
    other = 1 - half
    base = s - half
    partner = base + other
    has_low, has_high = s >= stride, s < spaces - stride
    rows = pl.ds(PAD, ny)

    barrier = pltpu.get_barrier_semaphore()

    def place(space, tm):
        return {"space": space, "tm": tm}

    zero_rows = jnp.zeros((PAD, nx), jnp.float32)
    for heat in (heat_a, heat_b, heat_c):
        for layer in range(2 * depth + 4):
            heat[layer, pl.ds(0, PAD), :] = zero_rows
            heat[layer, pl.ds(PAD + ny, PAD), :] = zero_rows
        for layer in (0, 1, thick + 2, thick + 3):
            heat[layer, rows, :] = jnp.zeros((ny, nx), jnp.float32)

    friends = [
        (t >= 0, partner, t), (t >= 0, s, mate), (t >= 0, partner, mate),
        (distant, base, t - 2), (distant, base + 1, t - 2),
        (sender, base, t + 2), (sender, base + 1, t + 2),
        (jnp.logical_and(odd, t + 1 < blocks), s, t + 1),
        (jnp.logical_and(jnp.logical_not(odd), t > 0), s, t - 1),
        (has_low, s - stride, t), (has_high, s + stride, t),
    ]
    count = 0
    for there, layer in ((has_low, 0), (has_high, thick + 1)):
        @pl.when(jnp.logical_not(there))
        def _(layer=layer):
            for ref in (dens, prog, mobile):
                ref[layer] = jnp.zeros((ny, nx), jnp.float32)

    for there, space, tm in friends:
        @pl.when(there)
        def _(space=space, tm=tm):
            pl.semaphore_signal(barrier, 1, device_id=place(space, tm), device_id_type=MESH)
        count = count + there.astype(jnp.int32)

    def piece_of(source, piece):
        if piece == 0:
            return source * (depth - EDGE), EDGE
        return (1 - source) * EDGE, depth - EDGE

    def landing(field, where, low, layers):
        start = where * depth + low
        if field == 0:
            return heat_a.at[pl.ds(start + 2, layers), rows, :]
        return (dens, prog)[field - 1].at[pl.ds(start + 1, layers)]

    def start_copy(source, chain, field, piece, tm):
        low, layers = piece_of(source, piece)
        return pltpu.make_async_remote_copy(
            guess.at[chain, field, pl.ds(low, layers)], landing(field, source, low, layers),
            start_send.at[chain, field, piece], start_recv.at[source, field, piece],
            device_id=place(base + chain, tm), device_id_type=MESH)

    def own_start(field, low, layers, mine):
        some = pl.ds(low, layers)
        return guess.at[half if mine else other, field, some], initial.at[field, some]

    def local_copy(field, source):
        return pltpu.make_async_copy(
            own_start(field, 0, depth, True)[source], landing(field, half, 0, depth), local_sem.at[field])

    def swap_copy(field, piece, source):
        low, layers = piece_of(half, piece)
        return pltpu.make_async_remote_copy(
            own_start(field, low, layers, False)[source], landing(field, half, low, layers),
            first_send.at[field, piece], start_recv.at[half, field, piece],
            device_id=place(partner, t), device_id_type=MESH)

    def send_swap(source):
        for piece in range(2):
            for field in range(3):
                swap_copy(field, piece, source).start()

    map_copy = pltpu.make_async_copy(coarse, maps, map_sem)

    @pl.when(jnp.logical_not(odd))
    def _():
        for field in range(3):
            local_copy(field, 0).start()

    @pl.when(opening)
    def _():
        for field in range(3):
            local_copy(field, 1).start()

    table = jnp.broadcast_to(mobility[...], (8, nx))

    def look_up(layer, carry):
        for row in range(0, ny, 8):
            index = sites[layer, pl.ds(row, 8), :]
            found = jnp.take_along_axis(table, index, axis=1, mode="promise_in_bounds")
            own_mobile[layer, pl.ds(row, 8), :] = found
            mobile[layer + 1 + offset, pl.ds(row, 8), :] = found
        return carry

    lax.fori_loop(0, depth, look_up, 0)
    quarter = depth // 2

    def mobile_copy():
        return pltpu.make_async_remote_copy(
            own_mobile.at[pl.ds(share * quarter, quarter)],
            mobile.at[pl.ds(1 + half * depth + share * quarter, quarter)], mob_send.at[0], mob_recv.at[0],
            device_id=place(partner, t), device_id_type=MESH)

    def mobile_pass(which):
        some = mobile.at[pl.ds(1 + other * depth + which * quarter, quarter)]
        return pltpu.make_async_remote_copy(
            some, some, mob_send.at[1], mob_recv.at[1],
            device_id=place(s, mate), device_id_type=MESH)

    pl.semaphore_wait(barrier, count)

    def wait_sent(pieces):
        @pl.when(sender)
        def _():
            for field in range(3):
                for chain in range(2):
                    for piece in pieces:
                        start_copy(half, chain, field, piece, t + 2).wait_send()

    def wait_start(piece):
        for field in range(3):
            start_copy(other, 0, field, piece, t).wait_recv()

        @pl.when(distant)
        def _():
            for field in range(3):
                start_copy(half, 0, field, piece, t).wait_recv()

    mobile_copy().start()

    @pl.when(jnp.logical_not(odd))
    def _():
        send_swap(0)

    @pl.when(sender)
    def _():
        for piece in range(2):
            for field in range(3):
                for chain in range(2):
                    start_copy(half, chain, field, piece, t + 2).start()

    mobile_copy().wait()
    mobile_pass(share).start()
    map_copy.start()
    wait_sent((0,))

    @pl.when(opening)
    def _():
        send_swap(1)

    @pl.when(near)
    def _():
        for field in range(3):
            local_copy(field, 0).wait()

    wait_start(0)

    part = ny // CHUNKS

    def halo(heat, parity, side, far, chunk):
        source, target, space = (
            (2 + far, thick + 2 + far, s - stride), (thick + 1 - far, 1 - far, s + stride))[side]
        some = pl.ds(PAD + chunk * part, part)
        return pltpu.make_async_remote_copy(
            heat.at[source, some, :], heat.at[target, some, :],
            halo_send.at[parity, side, far, chunk], halo_recv.at[parity, side, far, chunk],
            device_id=place(space, t), device_id_type=MESH)

    def send_halo(heat, parity, side, far, chunk, go):
        @pl.when(jnp.logical_and((has_low, has_high)[side], go))
        def _():
            halo(heat, parity, side, far, chunk).start()

    def wait_halo(heat, parity, side, far, chunk):
        @pl.when((has_low, has_high)[side])
        def _():
            halo(heat, parity, side, far, chunk).wait_send()
            halo(heat, parity, 1 - side, far, chunk).wait_recv()

    for far in range(2):
        for side in range(2):
            for chunk in range(CHUNKS):
                send_halo(heat_a, 0, side, far, chunk, True)
    edges = (dens, prog, mobile)

    def edge(number, side):
        ref = edges[number]
        source, target, space = ((1, thick + 1, s - stride), (thick, 0, s + stride))[side]
        return pltpu.make_async_remote_copy(
            ref.at[source], ref.at[target], edge_send.at[number, side], edge_recv.at[number, side],
            device_id=place(space, t), device_id_type=MESH)

    def send_edges(numbers):
        for side in range(2):
            @pl.when((has_low, has_high)[side])
            def _(side=side):
                for number in numbers:
                    edge(number, side).start()

    send_edges((0, 1))

    mobile_pass(1 - share).wait_recv()

    send_edges((2,))

    wait_start(1)

    for side in range(2):
        @pl.when((has_low, has_high)[side])
        def _(side=side):
            for number in range(3):
                edge(number, side).wait_send()
                edge(number, 1 - side).wait_recv()

    lane = lax.broadcasted_iota(jnp.int32, (ROWS, nx), 1)
    not_first, not_last = lane > 0, lane < nx - 1

    def update(source, target, layer, skip=0):
        for row in range(0, ny, ROWS):
            here = pl.ds(row, ROWS)
            center = source[layer, pl.ds(PAD + row, ROWS), :]
            density = dens[layer - 1, here, :]
            progress = prog[layer - 1, here, :]
            square = density * density
            driving = square * pl.reciprocal(1.0 + square)
            growth = mobile[layer - 1, here, :] * (1.0 + 0.5 * jnp.tanh(center)) * driving
            growth = growth * (1.0 - jnp.tanh(progress))
            if target is not None:
                around = source[layer, pl.ds(PAD + row - 1, ROWS), :] + source[layer, pl.ds(PAD + row + 1, ROWS), :]
                if skip != -1:
                    around = around + source[layer - 1, pl.ds(PAD + row, ROWS), :]
                if skip != 1:
                    around = around + source[layer + 1, pl.ds(PAD + row, ROWS), :]
                left = jnp.where(not_first, pltpu.roll(center, 1, 1), 0.0)
                right = jnp.where(not_last, pltpu.roll(center, nx - 1, 1), 0.0)
                around = around + (left + right)
                target[layer, pl.ds(PAD + row, ROWS), :] = (
                    (1.0 - 6.0 * diffusion_number) * center + diffusion_number * around + heat_release * growth)
            dens[layer - 1, here, :] = density * ((1.0 - hardening) - growth) + hardening * saturation
            prog[layer - 1, here, :] = progress + growth

    def add_halo(source, middle, target, outer, inner, step, chunk):
        for row in range(chunk * part, (chunk + 1) * part, SOME):
            here = pl.ds(PAD + row, SOME)
            value = middle[inner, here, :] + diffusion_number * source[outer, here, :]
            middle[inner, here, :] = value
            target[inner + step, here, :] = target[inner + step, here, :] + diffusion_number * value

    ends = ((0, 2, 1), (1, thick + 1, -1))

    def fine_copy(field, where, layer, slot):
        start = where * depth + layer
        source = heat_a.at[start + 2, rows, :] if field == 0 else (dens, prog)[field - 1].at[start + 1]
        return pltpu.make_async_remote_copy(
            source, fine.at[slot, field, layer], back_send.at[where, field, layer], back_recv.at[slot, field, layer],
            device_id=place(base + where, mate), device_id_type=MESH)

    def send_fine(where, piece):
        low, layers = piece_of(where, piece)
        for layer in range(layers):
            for field in range(3):
                fine_copy(field, where, low + layer, half).start()

    def cycle(source, middle, target, parity, order, go):
        for layer in range(3, thick + 1):
            update(source, middle, layer)
        for _, inner, step in order:
            update(source, middle, inner, -step)
        for layer in range(4, thick):
            update(middle, target, layer)
        for _, inner, step in order:
            update(middle, target, inner + step, -step)
        if go is not True:
            @pl.when(jnp.logical_and(jnp.logical_not(go), both_ways))
            def _():
                send_fine(other, 1)

            @pl.when(jnp.logical_not(go))
            def _():
                send_fine(half, 1)
        for side, inner, step in order:
            for chunk in range(CHUNKS):
                wait_halo(source, parity, side, 0, chunk)
                add_halo(source, middle, target, inner - step, inner, step, chunk)
                send_halo(target, 1 - parity, side, 1, chunk, go)
            update(source, middle, inner - step, -step)
            update(middle, target, inner, -step)
            for chunk in range(CHUNKS):
                @pl.when((has_low, has_high)[side])
                def _(side=side, inner=inner, step=step, chunk=chunk):
                    wait_halo(source, parity, side, 1, chunk)
                    add_halo(source, middle, target, inner - 2 * step, inner - step, step, chunk)
                send_halo(target, 1 - parity, side, 0, chunk, go)
            if go is not True:
                mine = jnp.logical_or(both_ways, half == side)

                @pl.when(jnp.logical_and(jnp.logical_not(go), mine))
                def _(side=side):
                    send_fine(side, 0)
        for _, inner, step in order:
            update(middle, None, inner - step)

    total = 2 * M // 4

    def state(field, layer):
        if field == 0:
            return heat_a[layer + 2, rows, :]
        return (dens, prog)[field - 1][layer + 1]

    def keep(layer, carry):
        for where in range(2):
            for field in range(3):
                relaxed_out[where, field, layer] = state(field, where * depth + layer)
        return carry

    def relaxed_copy(where, slot):
        return pltpu.make_async_remote_copy(
            relaxed_out.at[where], relaxed.at[slot], relaxed_send.at[where], relaxed_recv.at[slot],
            device_id=place(base + where, mate), device_id_type=MESH)

    def four_steps(index, carry):
        @pl.when(index == total // 2)
        def _():
            lax.fori_loop(0, depth, keep, 0)
            relaxed_copy(half, half).start()

            @pl.when(both_ways)
            def _():
                relaxed_copy(other, half).start()

        cycle(heat_a, heat_b, heat_c, 0, ends, True)
        cycle(heat_c, heat_b, heat_a, 1, ends, index < total - 1)
        return carry

    lax.fori_loop(0, total, four_steps, 0)

    map_copy.wait()
    wait_sent((1,))
    mobile_pass(share).wait_send()

    @pl.when(near)
    def _():
        for field in range(3):
            for piece in range(2):
                swap_copy(field, piece, 0).wait_send()

    relaxed_copy(half, half).wait_send()

    @pl.when(both_ways)
    def _():
        relaxed_copy(other, half).wait_send()

    relaxed_copy(half, half).wait_recv()

    @pl.when(later)
    def _():
        relaxed_copy(half, other).wait_recv()

    slab = ny // PARTS

    def chain_copy(layer, piece, tm):
        some = pl.ds(piece * slab, slab)
        return pltpu.make_async_remote_copy(
            out.at[1, :, layer, some, :], arriving.at[:, layer, some, :],
            chain_send.at[layer, piece], chain_recv.at[layer, piece],
            device_id=place(s, tm), device_id_type=MESH)

    def result_copy(layer):
        return pltpu.make_async_copy(out.at[:, :, layer], result.at[:, :, layer], out_sem.at[layer])

    def link(index, carry):
        layer = lax.rem(index + other * EDGE, depth)
        for field in range(3):
            fine_copy(field, half, layer, half).wait_recv()

        @pl.when(first)
        def _():
            for field in range(3):
                out[0, field, layer] = relaxed[half, field, layer]
                out[1, field, layer] = fine[half, field, layer]
            for piece in range(PARTS):
                chain_copy(layer, piece, t + 1).start()

        @pl.when(later)
        def _():
            for field in range(3):
                fine_copy(field, half, layer, other).wait_recv()
            for piece in range(PARTS):
                chain_copy(layer, piece, t).wait_recv()
                for row in range(piece * slab, (piece + 1) * slab, ROWS):
                    here = pl.ds(row, ROWS)
                    value = [arriving[field, layer, here, :] for field in range(3)]
                    for slot in range(2):
                        change = [value[field] - relaxed[slot, field, layer, here, :] for field in range(3)]
                        value = [
                            fine[slot, r, layer, here, :]
                            + (maps[r, 0, layer, here, :] * change[0] + maps[r, 1, layer, here, :] * change[1]
                               + maps[r, 2, layer, here, :] * change[2])
                            for r in range(3)
                        ]
                        for field in range(3):
                            out[slot, field, layer, here, :] = value[field]

                @pl.when(jnp.logical_not(last))
                def _(piece=piece):
                    chain_copy(layer, piece, t + 1).start()

        result_copy(layer).start()
        return carry

    lax.fori_loop(0, depth, link, 0)

    for layer in range(depth):
        result_copy(layer).wait()

    @pl.when(jnp.logical_not(last))
    def _():
        for layer in range(depth):
            for piece in range(PARTS):
                chain_copy(layer, piece, t + 1).wait_send()

    for layer in range(depth):
        for field in range(3):
            fine_copy(field, half, layer, half).wait_send()

    @pl.when(both_ways)
    def _():
        for layer in range(depth):
            for field in range(3):
                fine_copy(field, other, layer, half).wait_send()


def shards(spaces, blocks, initial, guess, coarse_map, sites, mobility):
    depth, ny, nx = sites.shape
    thick = 2 * depth
    heat = pltpu.VMEM((thick + 4, ny + 2 * PAD, nx), jnp.float32)
    wide = pltpu.VMEM((thick + 2, ny, nx), jnp.float32)
    both = pltpu.VMEM((2, 3, depth, ny, nx), jnp.float32)
    one = pltpu.VMEM((3, depth, ny, nx), jnp.float32)
    dma = pltpu.SemaphoreType.DMA
    vmem = pl.BlockSpec(memory_space=pltpu.VMEM)
    hbm = pl.BlockSpec(memory_space=pl.ANY)
    return pl.pallas_call(
        functools.partial(kernel, spaces, blocks),
        out_shape=jax.ShapeDtypeStruct(guess.shape, jnp.float32),
        in_specs=[hbm, hbm, hbm, vmem, vmem],
        out_specs=hbm,
        scratch_shapes=[
            heat, heat, heat, wide, wide, wide, pltpu.VMEM((depth, ny, nx), jnp.float32),
            both, both, both, both, one, pltpu.VMEM(coarse_map.shape, jnp.float32),
            dma((2, 3, 2)), dma((2, 3, 2)), dma((3,)), dma((3, 2)), dma((2,)), dma((2,)),
            dma((2, 2, 2, CHUNKS)), dma((2, 2, 2, CHUNKS)), dma((3, 2)), dma((3, 2)),
            dma((2,)), dma((2,)), dma((2, 3, depth)), dma((2, 3, depth)), dma((depth, PARTS)), dma((depth, PARTS)), dma, dma((depth,)),
        ],
        compiler_params=pltpu.CompilerParams(
            collective_id=0, has_side_effects=True, vmem_limit_bytes=60 * 1024 * 1024),
    )(initial, guess, coarse_map, sites, mobility.reshape(1, -1))


def solution(mesh):
    placed = (
        P(None, "space", None, None),
        P("tm", None, "space", None, None),
        P(None, None, "space", None, None),
        P("space", None, None),
        P(),
    )
    return jax.shard_map(
        functools.partial(shards, mesh.shape["space"], mesh.shape["tm"]),
        mesh=mesh,
        in_specs=placed,
        out_specs=P("tm", None, "space", None, None),
        check_vma=False,
    )
```
